32 devices in a mesh: row: 4 (over y, core), col: 8 (over z, x).
Axes of the slice: x: 2, y: 2, z: 4, core: 2. Of those that a mesh axis runs over, the one named last changes fastest.
Arguments:
- inputs: bfloat16 [1024, 6144], P('col', 'row'), may hold values from -1200 to 1200
- norm_gain: float32 [6144], P('row'), may hold values from 0.5 to 9
- weight_in: bfloat16 [6144, 24576], P('row', 'col'), may hold values from -1 to 1
- weight_out: bfloat16 [24576, 6144], P('col', 'row'), may hold values from -0.0390625 to 0.0390625
- cotangent: bfloat16 [1024, 6144], P('col', 'row'), may hold values from -4 to 4
Outputs:
- branch: bfloat16 [1024, 6144], P('col', 'row')
- input_gradient: bfloat16 [1024, 6144], P('col', 'row')
- in_gradient: float32 [6144, 24576], P('row', 'col')
- out_gradient: float32 [24576, 6144], P('col', 'row')
- gain_gradient: float32 [6144], P('row')
The draws below stay inside these ranges and needn't reach their ends.
All inputs are finite; a program needn't handle non-finite values.
Results may differ from the reference program's by a relative error of at most 0.039.
Values may be sent and summed in bfloat16 or wider, within the bound.
A program may use at most 128 MiB of HBM per device.

```python
import jax
import jax.numpy as jnp
from jax import lax

D = 6144
FF = 24576
TOKENS = 1024
N_ROW = 4
N_COL = 8


def draw_inputs(key, part):
    key = jax.random.fold_in(key, 11)
    first, second, third = jax.random.split(key, 3)
    rising = 3.0 ** (jnp.arange(D, dtype=jnp.float32) / (D - 1))
    column_scale = rising[None, :] * 10.0 ** (0.5 * jax.random.uniform(third, (1, D), jnp.float32))
    noise = jax.random.truncated_normal(first, -6.0, 6.0, (TOKENS, D), jnp.float32)
    row_scale = 10.0 ** jax.random.uniform(second, (TOKENS, 1), jnp.float32)
    values = noise * row_scale * column_scale
    return values.astype(jnp.bfloat16)


def draw_norm_gain(key, part):
    key = jax.random.fold_in(key, 12)
    position = jnp.arange(D, dtype=jnp.float32) / (D - 1)
    factor = jax.random.uniform(key, (D,), jnp.float32, minval=0.6, maxval=1.4)
    values = factor * 3.0 ** position
    return values.astype(jnp.float32)


def draw_weight_in(key, part):
    key = jax.random.fold_in(key, 13)
    first, second = jax.random.split(key, 2)
    shared = jax.random.truncated_normal(second, -3.0, 3.0, (1, FF), jnp.float32)
    noise = jax.random.truncated_normal(first, -4.0, 4.0, (D, FF), jnp.float32)
    values = (noise + shared) * (1.0 / jnp.sqrt(jnp.float32(D)))
    return values.astype(jnp.bfloat16)


def shard_levels(key, shape, cuts, low, high):
    loudness, own = 1.0, jax.random.fold_in(key, 6)
    for dim, blocks in cuts:
        steps = jnp.exp(jax.random.uniform(jax.random.fold_in(own, dim), (blocks,), jnp.float32, low / len(cuts), high / len(cuts)))
        loudness = loudness * jnp.repeat(steps, shape[dim] // blocks).reshape([-1 if axis == dim else 1 for axis in range(len(shape))])
    return loudness


def gaussian(stream_key, shape, scale, limit, cuts=(), kind=jnp.bfloat16):
    loudness = shard_levels(stream_key, shape, cuts, -0.22, 0.18) if cuts else 1.0
    entries = jax.random.normal(stream_key, shape, jnp.float32) * scale * loudness
    return jnp.minimum(jnp.maximum(entries, -limit), limit).astype(kind)


def setup_inputs(seed: int = 0) -> dict:
    keys = jax.random.split(jax.random.key(seed), 6)
    return {
        "inputs": draw_inputs(jax.random.fold_in(keys[5], 71), 0),
        "norm_gain": draw_norm_gain(jax.random.fold_in(keys[5], 71), 0),
        "weight_in": draw_weight_in(jax.random.fold_in(keys[5], 71), 0),
        "weight_out": gaussian(keys[3], (FF, D), FF ** -0.5, 0.0390625, ((0, 8), (1, 4))),
        "cotangent": gaussian(keys[4], (TOKENS, D), 0.25, 4.0, ((0, 8), (1, 4))),
    }


epsilon = 1e-06

def gelu_value(value):
    return jax.nn.gelu(value, approximate=False)

def gelu_slope(value, upstream):
    return jax.vjp(gelu_value, value)[1](upstream)[0]

def rounded(term):
    return lax.optimization_barrier(term.astype(jnp.bfloat16)).astype(jnp.float32)

def block_sum(left, right, blocks, right_rows):
    width = left.shape[1] // blocks
    out_cols = right.shape[1] if right_rows else right.shape[0]

    def advance(block, total):
        start = (block * width).astype(jnp.int32)
        piece = lax.dynamic_slice_in_dim(left, start, width, 1)
        if right_rows:
            other = lax.dynamic_slice_in_dim(right, start, width, 0)
            term = jnp.dot(piece, other, preferred_element_type=jnp.float32)
        else:
            other = lax.dynamic_slice_in_dim(right, start, width, 1)
            term = lax.dot_general(piece, other, (((1,), (1,)), ((), ())), preferred_element_type=jnp.float32)
        return total + rounded(term)
    return lax.fori_loop(0, blocks, advance, jnp.zeros((left.shape[0], out_cols), jnp.float32))

def reference(inputs, norm_gain, weight_in, weight_out, cotangent):
    floats = inputs.astype(jnp.float32)
    center = lax.optimization_barrier(jnp.sum(floats, axis=1)) / D
    meansq = lax.optimization_barrier(jnp.sum(floats * floats, axis=1)) / D
    spread = lax.rsqrt(meansq - center * center + epsilon)
    normed = (floats - center[:, None]) * spread[:, None]
    scaled = (normed * norm_gain[None, :]).astype(jnp.bfloat16)
    hidden = block_sum(scaled, weight_in, N_ROW, True)
    active = gelu_value(hidden).astype(jnp.bfloat16)
    branch = block_sum(active, weight_out, N_COL, True).astype(jnp.bfloat16)
    active_gradient = block_sum(cotangent, weight_out, N_ROW, False)
    hidden_gradient = gelu_slope(hidden, active_gradient).astype(jnp.bfloat16)
    out_gradient = lax.dot_general(active, cotangent, (((0,), (0,)), ((), ())), preferred_element_type=jnp.float32)
    in_gradient = lax.dot_general(scaled, hidden_gradient, (((0,), (0,)), ((), ())), preferred_element_type=jnp.float32)
    normed_gradient = block_sum(hidden_gradient, weight_in, N_COL, False)
    gain_gradient = lax.optimization_barrier(jnp.sum(normed_gradient * normed, axis=0))
    scaled_gradient = normed_gradient * norm_gain[None, :]
    mean_gradient = lax.optimization_barrier(jnp.sum(scaled_gradient, axis=1)) / D
    mean_cross = lax.optimization_barrier(jnp.sum(scaled_gradient * normed, axis=1)) / D
    input_gradient = spread[:, None] * (scaled_gradient - mean_gradient[:, None] - normed * mean_cross[:, None])
    return (branch, input_gradient.astype(jnp.bfloat16), in_gradient, out_gradient, gain_gradient)
```

```python
import jax
import jax.numpy as jnp
from jax import lax
from jax.sharding import PartitionSpec as P

epsilon = 1e-06


def gelu_value(value):
    return jax.nn.gelu(value, approximate=False)


def gelu_slope(value, upstream):
    return jax.vjp(gelu_value, value)[1](upstream)[0]


def shifted(value, axis, outer, inner, outer_step, inner_step):
    pairs = []
    for first in range(outer):
        for second in range(inner):
            source = ((first + outer_step) % outer) * inner + (second + inner_step) % inner
            pairs.append((source, first * inner + second))
    return lax.ppermute(value, axis, pairs)


def make_per_device(rows, cols):
    core_n = 2
    y_n = rows // core_n
    z_n = 4 if cols % 4 == 0 else 1
    x_n = cols // z_n

    def along_z(value, step):
        return value if step % z_n == 0 else shifted(value, "col", z_n, x_n, step, 0)

    def along_x(value, step):
        return value if step % x_n == 0 else shifted(value, "col", z_n, x_n, 0, step)

    def along_y(value, step):
        return value if step % y_n == 0 else shifted(value, "row", y_n, core_n, step, 0)

    def along_core(value, step):
        return value if step % core_n == 0 else shifted(value, "row", y_n, core_n, 0, step)

    def gather_col(block):
        chunks = []
        for dz in range(z_n):
            piece = along_z(block, dz)
            chunks.append(jnp.concatenate([along_x(piece, dx) for dx in range(x_n)], axis=0))
        return chunks

    def send_col(partial, dz):
        blocks = jnp.split(partial, x_n, axis=0)
        total = sum(along_x(blocks[dx], -dx).astype(jnp.float32) for dx in range(x_n))
        return along_z(total.astype(jnp.bfloat16), -dz).astype(jnp.float32)

    def scatter_row(partial):
        place = lax.axis_index("row")
        y, core = place // core_n, place % core_n
        half = partial.shape[0] // core_n
        total = 0.0
        for step in range(core_n):
            part = lax.dynamic_slice_in_dim(partial, ((core + step) % core_n) * half, half, 0)
            total = total + along_core(part, -step).astype(jnp.float32)
        total = total.astype(jnp.bfloat16)
        quarter = half // y_n
        result = 0.0
        for step in range(y_n):
            part = lax.dynamic_slice_in_dim(total, ((y + step) % y_n) * quarter, quarter, 0)
            result = result + along_y(part, -step).astype(jnp.float32)
        return result

    def gather_row(part):
        place = lax.axis_index("row")
        y, core = place // core_n, place % core_n
        pieces = [along_y(part, step) for step in range(y_n)]
        half = jnp.concatenate([lax.select_n((k - y) % y_n, *pieces) if y_n > 1 else part for k in range(y_n)], axis=0)
        pieces = [along_core(half, step) for step in range(core_n)]
        return jnp.concatenate([lax.select_n((k - core) % core_n, *pieces) for k in range(core_n)], axis=0)

    def per_device(inputs, norm_gain, weight_in, weight_out, cotangent):
        width = inputs.shape[1] * rows
        floats = inputs.astype(jnp.float32)
        stats = lax.psum(jnp.stack([jnp.sum(floats, axis=1), jnp.sum(floats * floats, axis=1)]), "row")
        center = stats[0] / width
        spread = lax.rsqrt(stats[1] / width - center * center + epsilon)
        normed = (floats - center[:, None]) * spread[:, None]
        scaled = (normed * norm_gain[None, :]).astype(jnp.bfloat16)

        cot_chunks = gather_col(cotangent)
        scaled_chunks = gather_col(scaled)
        back = [
            scatter_row(
                lax.dot_general(c, weight_out, (((1,), (1,)), ((), ())), preferred_element_type=jnp.float32).astype(jnp.bfloat16)
            )
            for c in cot_chunks
        ]
        hidden = [
            scatter_row(jnp.dot(s, weight_in, preferred_element_type=jnp.float32).astype(jnp.bfloat16)) for s in scaled_chunks
        ]
        active = [gather_row(gelu_value(h).astype(jnp.bfloat16)) for h in hidden]
        slope = [gather_row(gelu_slope(h, b).astype(jnp.bfloat16)) for h, b in zip(hidden, back)]

        branch = 0.0
        for dz in range(z_n):
            branch = branch + send_col(
                jnp.dot(active[dz], weight_out, preferred_element_type=jnp.float32).astype(jnp.bfloat16), dz
            )
        normed_gradient = 0.0
        for dz in range(z_n):
            normed_gradient = normed_gradient + send_col(
                lax.dot_general(
                    slope[dz], weight_in, (((1,), (1,)), ((), ())), preferred_element_type=jnp.float32
                ).astype(jnp.bfloat16),
                dz,
            )
        out_gradient = lax.dot_general(
            jnp.concatenate(active), jnp.concatenate(cot_chunks), (((0,), (0,)), ((), ())), preferred_element_type=jnp.float32
        )
        in_gradient = lax.dot_general(
            jnp.concatenate(scaled_chunks), jnp.concatenate(slope), (((0,), (0,)), ((), ())), preferred_element_type=jnp.float32
        )
        gain_gradient = lax.psum(jnp.sum(normed_gradient * normed, axis=0), "col")
        scaled_gradient = normed_gradient * norm_gain[None, :]
        sums = lax.psum(jnp.stack([jnp.sum(scaled_gradient, axis=1), jnp.sum(scaled_gradient * normed, axis=1)]), "row") / width
        input_gradient = spread[:, None] * (scaled_gradient - sums[0][:, None] - normed * sums[1][:, None])
        return (
            branch.astype(jnp.bfloat16),
            input_gradient.astype(jnp.bfloat16),
            in_gradient,
            out_gradient,
            gain_gradient,
        )

    return per_device


def solution(mesh):
    in_specs = (P("col", "row"), P("row"), P("row", "col"), P("col", "row"), P("col", "row"))
    out_specs = (P("col", "row"), P("col", "row"), P("row", "col"), P("col", "row"), P("row"))
    per_device = make_per_device(mesh.shape["row"], mesh.shape["col"])
    return jax.shard_map(per_device, mesh=mesh, in_specs=in_specs, out_specs=out_specs, check_vma=False)
```

```python
import functools

import jax
import jax.numpy as jnp
from jax import lax
from jax.experimental import pallas as pl
from jax.experimental.pallas import tpu as pltpu
from jax.sharding import PartitionSpec as P

MESH = pl.DeviceIdType.MESH
CORES = 2
LANES = 128
epsilon = 1e-06
ROOT_HALF = 0.7071067811865476
ROOT_TWO_PI = 0.3989422804014327
ROWS_ROWS = (((1,), (1,)), ((), ()))
ROWS_COLS = (((1,), (0,)), ((), ()))


def tile_of(size):
    return 512 if size % 512 == 0 else 256 if size % 256 == 0 else 128


def layer_kernel(
    rows, y_n, z_n, x_n,
    inputs, gain, weight_in, weight_out, cotangent,
    branch, input_gradient, gain_gradient, cot_all, scl_all, act_all, slo_all,
    w_in, w_out, part, core_in, y_in, own, lhs, x_in, z_in, scaled, stats, sums, gains,
    ag_s, ag_r, rc_s, rc_r, ry_s, ry_r, ay_s, ay_r, ac_s, ac_r, xs_s, xs_r, zs_s, zs_r,
    st_s, st_r, gn_s, gn_r, load, wload, keep,
):
    block, d = inputs.shape
    ff = w_in.shape[1]
    tokens = x_n * block
    half = tokens // CORES
    quarter = half // y_n
    cols = z_n * x_n
    width = d * rows
    row = lax.axis_index("row")
    col = lax.axis_index("col")
    y, core = row // CORES, row % CORES
    z, x = col // x_n, col % x_n

    def at_z(step):
        return (row, lax.rem(z + step + z_n, z_n) * x_n + x)

    def at_x(step):
        return (row, z * x_n + lax.rem(x + step + x_n, x_n))

    def at_y(step):
        return (lax.rem(y + step, y_n) * CORES + core, col)

    other_core = (y * CORES + 1 - core, col)

    def remote(src, dst, send, recv, device):
        return pltpu.make_async_remote_copy(
            src_ref=src, dst_ref=dst, send_sem=send, recv_sem=recv, device_id=device, device_id_type=MESH
        )

    def take(src, dst):
        copy = pltpu.make_async_copy(src, dst, load)
        copy.start()
        copy.wait()

    barrier = pltpu.get_barrier_semaphore()
    for step in range(1, rows):
        pl.semaphore_signal(barrier, inc=1, device_id=(lax.rem(row + step, rows), col), device_id_type=MESH)
    for step in range(1, cols):
        pl.semaphore_signal(barrier, inc=1, device_id=(row, lax.rem(col + step, cols)), device_id_type=MESH)
    weight_loads = [
        pltpu.make_async_copy(weight_out, w_out, wload.at[0]),
        pltpu.make_async_copy(weight_in, w_in, wload.at[1]),
    ]
    for copy in weight_loads:
        copy.start()
    pl.semaphore_wait(barrier, rows + cols - 2)

    gathered = (cot_all, scl_all)
    spread_out = (act_all, slo_all)

    def block_rows(dz, dx):
        return pl.ds(dz * tokens + dx * block, block)

    def z_send(a, dz, src):
        return remote(src, gathered[a].at[block_rows(dz, 0)], ag_s.at[a, dz, 0], ag_r.at[a, dz, 0], at_z(-dz))

    def x_send(a, dz, dx, src):
        return remote(src, gathered[a].at[block_rows(dz, dx)], ag_s.at[a, dz, dx], ag_r.at[a, dz, dx], at_x(-dx))

    def begin(a, src):
        for dx in range(1, x_n):
            x_send(a, 0, dx, src).start()
        if z_n > 1:
            z_send(a, 1, src).start()
        pltpu.make_async_copy(src, gathered[a].at[block_rows(0, 0)], keep.at[a]).start()

    def forward(a, dz, src):
        z_send(a, dz, src).wait_recv()
        for dx in range(1, x_n):
            x_send(a, dz, dx, gathered[a].at[block_rows(dz, 0)]).start()
        if dz + 1 < z_n:
            z_send(a, dz + 1, src).start()

    begin(0, cotangent)

    floats = inputs[...].astype(jnp.float32)
    lane = lax.broadcasted_iota(jnp.int32, (block, LANES), 1)

    def pair(first, second):
        return jnp.where(lane == 0, first, jnp.where(lane == 1, second, 0.0))

    def exchange(use):
        for step in range(1, rows):
            remote(
                stats.at[use, 0], stats.at[use, step], st_s.at[use, step], st_r.at[use, step],
                (lax.rem(row + step, rows), col),
            ).start()
        total = stats[use, 0]
        for step in range(1, rows):
            remote(
                stats.at[use, 0], stats.at[use, step], st_s.at[use, step], st_r.at[use, step],
                (lax.rem(row + step, rows), col),
            ).wait()
            total = total + stats[use, step]
        total = total / width
        return (
            jnp.sum(jnp.where(lane == 0, total, 0.0), axis=1, keepdims=True),
            jnp.sum(jnp.where(lane == 1, total, 0.0), axis=1, keepdims=True),
        )

    stats[0, 0] = pair(jnp.sum(floats, axis=1, keepdims=True), jnp.sum(floats * floats, axis=1, keepdims=True))
    center, meansq = exchange(0)
    spread = lax.rsqrt(meansq - center * center + epsilon)
    sums[0] = jnp.broadcast_to(center, (block, LANES))
    sums[1] = jnp.broadcast_to(spread, (block, LANES))
    scaled[...] = ((floats - center) * spread * gain[...]).astype(jnp.bfloat16)
    begin(1, scaled)

    def core_copy(a, g):
        return remote(
            part.at[a, g, pl.ds(pl.multiple_of((1 - core) * half, half), half)], core_in.at[a, g],
            rc_s.at[a, g], rc_r.at[a, g], other_core,
        )

    def y_copy(a, g, step):
        start = core * half + lax.rem(y + step, y_n) * quarter
        return remote(
            part.at[a, g, pl.ds(pl.multiple_of(start, quarter), quarter)], y_in.at[a, g, step - 1],
            ry_s.at[a, g, step], ry_r.at[a, g, step], at_y(step),
        )

    def multiply(right, dims, out_cols, store):
        tile = tile_of(out_cols)

        @pl.loop(0, out_cols // tile)
        def _(n):
            here = pl.ds(pl.multiple_of(n * tile, tile), tile)
            left = lhs[...] if store[2] == ff else lhs[:, :d]
            piece = right[here, :] if dims is ROWS_ROWS else right[:, here]
            value = lax.dot_general(left, piece, dims, preferred_element_type=jnp.float32).astype(jnp.bfloat16)
            a, g, _, offset = store
            part[a, g, :, pl.ds(pl.multiple_of(offset + n * tile, LANES), tile)] = value

    own_blocks = (cotangent, scaled)

    def project(a, g):
        if g == 0:
            pltpu.make_async_copy(own_blocks[a], gathered[a].at[block_rows(0, 0)], keep.at[a]).wait()
            weight_loads[a].wait()
        for dx in range(1, x_n):
            x_send(a, g, dx, own_blocks[a]).wait_recv()
        take(gathered[a].at[pl.ds(g * tokens, tokens)], lhs.at[:, pl.ds(0, d)])
        multiply(w_out if a == 0 else w_in, ROWS_ROWS if a == 0 else ROWS_COLS, ff, (a, g, d, 0))
        core_copy(a, g).start()

    def core_sum(a, g):
        core_copy(a, g).wait()
        mine = pl.ds(pl.multiple_of(core * half, half), half)
        tile = tile_of(ff)

        @pl.loop(0, ff // tile)
        def _(n):
            here = pl.ds(pl.multiple_of(n * tile, tile), tile)
            total = part[a, g, mine, here].astype(jnp.float32) + core_in[a, g, :, here].astype(jnp.float32)
            part[a, g, mine, here] = total.astype(jnp.bfloat16)

        for step in range(1, y_n):
            y_copy(a, g, step).start()

    def share_copy(a, g, step):
        start = g * tokens + core * half + y * quarter
        return remote(
            own.at[a, g], spread_out[a].at[pl.ds(pl.multiple_of(start, quarter), quarter)],
            ay_s.at[a, g, step], ay_r.at[a, g, step], at_y(step),
        )

    def share_keep(a, g):
        start = g * tokens + core * half + y * quarter
        return pltpu.make_async_copy(
            own.at[a, g], spread_out[a].at[pl.ds(pl.multiple_of(start, quarter), quarter)], ay_s.at[a, g, 0]
        )

    def activate(g):
        for a in range(2):
            for step in range(1, y_n):
                y_copy(a, g, step).wait()
        mine = pl.ds(pl.multiple_of(core * half + y * quarter, quarter), quarter)
        tile = tile_of(ff)

        @pl.loop(0, ff // tile)
        def _(n):
            here = pl.ds(pl.multiple_of(n * tile, tile), tile)
            back = part[0, g, mine, here].astype(jnp.float32)
            hidden = part[1, g, mine, here].astype(jnp.float32)
            for step in range(y_n - 1):
                back = back + y_in[0, g, step, :, here].astype(jnp.float32)
                hidden = hidden + y_in[1, g, step, :, here].astype(jnp.float32)
            cdf = 0.5 * (1.0 + lax.erf(hidden * ROOT_HALF))
            density = jnp.exp(-0.5 * hidden * hidden) * ROOT_TWO_PI
            own[0, g, :, here] = (hidden * cdf).astype(jnp.bfloat16)
            own[1, g, :, here] = (back * (cdf + hidden * density)).astype(jnp.bfloat16)

        for a in range(2):
            for step in range(1, y_n):
                share_copy(a, g, step).start()
            share_keep(a, g).start()

    def half_copy(a, g):
        here = pl.ds(pl.multiple_of(g * tokens + core * half, half), half)
        return remote(spread_out[a].at[here], spread_out[a].at[here], ac_s.at[a, g], ac_r.at[a, g], other_core)

    def pass_on(g):
        for a in range(2):
            for step in range(1, y_n):
                share_copy(a, g, step).wait()
            share_keep(a, g).wait()
            half_copy(a, g).start()

    def x_copy(a, g, dx):
        return remote(
            part.at[0, g, pl.ds(dx * block, block), pl.ds(a * d, d)], x_in.at[a, g, dx - 1],
            xs_s.at[a, g, dx], xs_r.at[a, g, dx], at_x(dx),
        )

    def z_copy(a, g):
        return remote(
            part.at[0, g, pl.ds(0, block), pl.ds(a * d, d)], z_in.at[a, g - 1], zs_s.at[a, g], zs_r.at[a, g], at_z(g)
        )

    def finish(a, g):
        half_copy(a, g).wait()
        take(spread_out[a].at[pl.ds(g * tokens, tokens)], lhs)
        multiply(w_out if a == 0 else w_in, ROWS_COLS if a == 0 else ROWS_ROWS, d, (0, g, ff, a * d))
        for dx in range(1, x_n):
            x_copy(a, g, dx).start()

    def x_sum(a, g):
        for dx in range(1, x_n):
            x_copy(a, g, dx).wait()
        if x_n > 1:
            total = part[0, g, :block, a * d : (a + 1) * d].astype(jnp.float32)
            for dx in range(1, x_n):
                total = total + x_in[a, g, dx - 1].astype(jnp.float32)
            part[0, g, :block, a * d : (a + 1) * d] = total.astype(jnp.bfloat16)
        if g:
            z_copy(a, g).start()

    for step in range(z_n + 4):
        for a in range(2):
            if step < z_n:
                project(a, step)
            if step + 1 < z_n:
                forward(a, step + 1, own_blocks[a])
        if step < z_n:
            for a in range(2):
                core_sum(a, step)
        if 0 <= step - 1 < z_n:
            activate(step - 1)
        if 0 <= step - 3 < z_n:
            for a in range(2):
                x_sum(a, step - 3)
        if 0 <= step - 2 < z_n:
            pass_on(step - 2)
            for a in range(2):
                finish(a, step - 2)

    def collected(a):
        total = part[0, 0, :block, a * d : (a + 1) * d].astype(jnp.float32)
        for g in range(1, z_n):
            z_copy(a, g).wait()
            total = total + z_in[a, g - 1].astype(jnp.float32)
        return total

    normed_gradient = collected(1)
    normed = (inputs[...].astype(jnp.float32) - sums[0][:, :1]) * sums[1][:, :1]
    gains[0] = jnp.broadcast_to(jnp.sum(normed_gradient * normed, axis=0, keepdims=True), gains.shape[1:])

    def gain_copy(step):
        return remote(gains.at[0], gains.at[step], gn_s.at[step], gn_r.at[step], (row, lax.rem(col + step, cols)))

    for step in range(1, cols):
        gain_copy(step).start()
    scaled_gradient = normed_gradient * gain[...]
    stats[1, 0] = pair(
        jnp.sum(scaled_gradient, axis=1, keepdims=True), jnp.sum(scaled_gradient * normed, axis=1, keepdims=True)
    )
    mean_gradient, mean_cross = exchange(1)
    input_gradient[...] = (sums[1][:, :1] * (scaled_gradient - mean_gradient - normed * mean_cross)).astype(jnp.bfloat16)
    branch[...] = collected(0).astype(jnp.bfloat16)
    total = gains[0]
    for step in range(1, cols):
        gain_copy(step).wait()
        total = total + gains[step]
    gain_gradient[...] = total
    for a in range(2):
        for dz in range(z_n):
            for dx in range(x_n):
                if dx:
                    x_send(a, dz, dx, own_blocks[a]).wait_send()
                elif dz:
                    z_send(a, dz, own_blocks[a]).wait_send()


def make_per_device(rows, cols):
    y_n = rows // CORES
    z_n = 4 if cols % 4 == 0 else 1
    x_n = cols // z_n

    def per_device(inputs, norm_gain, weight_in, weight_out, cotangent):
        block, d = inputs.shape
        ff = weight_in.shape[1]
        tokens = x_n * block
        half = tokens // CORES
        quarter = half // y_n
        every = z_n * tokens
        bf16, f32 = jnp.bfloat16, jnp.float32
        dma = pltpu.SemaphoreType.DMA
        vmem = pl.BlockSpec(memory_space=pltpu.VMEM)
        anywhere = pl.BlockSpec(memory_space=pl.ANY)

        def shape(*dims, dtype=bf16):
            return jax.ShapeDtypeStruct(dims, dtype)

        outs = pl.pallas_call(
            functools.partial(layer_kernel, rows, y_n, z_n, x_n),
            out_shape=(
                shape(block, d), shape(block, d), shape(8, d, dtype=f32),
                shape(every, d), shape(every, d), shape(every, ff), shape(every, ff),
            ),
            in_specs=[vmem, vmem, anywhere, anywhere, anywhere],
            out_specs=(vmem, vmem, vmem, anywhere, anywhere, anywhere, anywhere),
            scratch_shapes=[
                pltpu.VMEM((d, ff), bf16),
                pltpu.VMEM((ff, d), bf16),
                pltpu.VMEM((2, z_n, tokens, ff), bf16),
                pltpu.VMEM((2, z_n, half, ff), bf16),
                pltpu.VMEM((2, z_n, max(y_n - 1, 1), quarter, ff), bf16),
                pltpu.VMEM((2, z_n, quarter, ff), bf16),
                pltpu.VMEM((tokens, ff), bf16),
                pltpu.VMEM((2, z_n, max(x_n - 1, 1), block, d), bf16),
                pltpu.VMEM((2, max(z_n - 1, 1), block, d), bf16),
                pltpu.VMEM((block, d), bf16),
                pltpu.VMEM((2, rows, block, LANES), f32),
                pltpu.VMEM((2, block, LANES), f32),
                pltpu.VMEM((cols, 8, d), f32),
                dma((2, z_n, x_n)), dma((2, z_n, x_n)),
                dma((2, z_n)), dma((2, z_n)),
                dma((2, z_n, y_n)), dma((2, z_n, y_n)),
                dma((2, z_n, y_n)), dma((2, z_n, y_n)),
                dma((2, z_n)), dma((2, z_n)),
                dma((2, z_n, x_n)), dma((2, z_n, x_n)),
                dma((2, z_n)), dma((2, z_n)),
                dma((2, rows)), dma((2, rows)),
                dma((cols,)), dma((cols,)),
                dma, dma((2,)), dma((2,)),
            ],
            compiler_params=pltpu.CompilerParams(
                collective_id=0, has_side_effects=True, vmem_limit_bytes=62 * 1024 * 1024
            ),
            cost_estimate=pl.CostEstimate(
                flops=8 * every * d * ff, bytes_accessed=8 * d * ff, transcendentals=2 * every * ff // rows
            ),
        )(inputs, norm_gain[None, :], weight_in, weight_out, cotangent)
        branch, input_gradient, gain_gradient, cot_all, scl_all, act_all, slo_all = outs
        over_tokens = (((0,), (0,)), ((), ()))
        out_gradient = lax.dot_general(act_all, cot_all, over_tokens, preferred_element_type=f32)
        in_gradient = lax.dot_general(scl_all, slo_all, over_tokens, preferred_element_type=f32)
        return branch, input_gradient, in_gradient, out_gradient, gain_gradient[0]

    return per_device


def solution(mesh):
    in_specs = (P("col", "row"), P("row"), P("row", "col"), P("col", "row"), P("col", "row"))
    out_specs = (P("col", "row"), P("col", "row"), P("row", "col"), P("col", "row"), P("row"))
    per_device = make_per_device(mesh.shape["row"], mesh.shape["col"])
    return jax.shard_map(per_device, mesh=mesh, in_specs=in_specs, out_specs=out_specs, check_vma=False)
```

```python
import functools

import jax
import jax.numpy as jnp
from jax import lax
from jax.experimental import pallas as pl
from jax.experimental.pallas import tpu as pltpu
from jax.sharding import PartitionSpec as P

MESH = pl.DeviceIdType.MESH
CORES = 2
LANES = 128
epsilon = 1e-06
ROOT_HALF = 0.7071067811865476
ROOT_TWO_PI = 0.3989422804014327
ROWS_ROWS = (((1,), (1,)), ((), ()))
ROWS_COLS = (((1,), (0,)), ((), ()))


def tile_of(size):
    return 512 if size % 512 == 0 else 256 if size % 256 == 0 else 128


def layer_kernel(
    rows, y_n, z_n, x_n,
    inputs, gain, weight_in, weight_out, cotangent,
    branch, input_gradient, gain_gradient, cot_all, scl_all, act_all, slo_all,
    w_in, w_out, part, core_in, y_in, own, lhs, x_in, z_in, scaled, stats, sums, gains,
    ag_s, ag_r, rc_s, rc_r, ry_s, ry_r, ay_s, ay_r, ac_s, ac_r, xs_s, xs_r, zs_s, zs_r,
    st_s, st_r, gn_s, gn_r, load, wload, keep,
):
    block, d = inputs.shape
    ff = w_in.shape[1]
    tokens = x_n * block
    half = tokens // CORES
    quarter = half // y_n
    cols = z_n * x_n
    width = d * rows
    row = lax.axis_index("row")
    col = lax.axis_index("col")
    y, core = row // CORES, row % CORES
    z, x = col // x_n, col % x_n

    def at_z(step):
        return (row, lax.rem(z + step + z_n, z_n) * x_n + x)

    def at_x(step):
        return (row, z * x_n + lax.rem(x + step + x_n, x_n))

    def at_y(step):
        return (lax.rem(y + step, y_n) * CORES + core, col)

    other_core = (y * CORES + 1 - core, col)

    def remote(src, dst, send, recv, device):
        return pltpu.make_async_remote_copy(
            src_ref=src, dst_ref=dst, send_sem=send, recv_sem=recv, device_id=device, device_id_type=MESH
        )

    def take(src, dst):
        copy = pltpu.make_async_copy(src, dst, load)
        copy.start()
        copy.wait()

    barrier = pltpu.get_barrier_semaphore()
    for step in range(1, rows):
        pl.semaphore_signal(barrier, inc=1, device_id=(lax.rem(row + step, rows), col), device_id_type=MESH)
    for step in range(1, cols):
        pl.semaphore_signal(barrier, inc=1, device_id=(row, lax.rem(col + step, cols)), device_id_type=MESH)
    weight_loads = [
        pltpu.make_async_copy(weight_out, w_out, wload.at[0]),
        pltpu.make_async_copy(weight_in, w_in, wload.at[1]),
    ]
    for copy in weight_loads:
        copy.start()
    pl.semaphore_wait(barrier, rows + cols - 2)

    gathered = (cot_all, scl_all)
    spread_out = (act_all, slo_all)

    def block_rows(dz, dx):
        return pl.ds(dz * tokens + dx * block, block)

    def z_send(a, dz, src):
        return remote(src, gathered[a].at[block_rows(dz, 0)], ag_s.at[a, dz, 0], ag_r.at[a, dz, 0], at_z(-dz))

    def x_send(a, dz, dx, src):
        return remote(src, gathered[a].at[block_rows(dz, dx)], ag_s.at[a, dz, dx], ag_r.at[a, dz, dx], at_x(-dx))

    def begin(a, src):
        for dx in range(1, x_n):
            x_send(a, 0, dx, src).start()
        if z_n > 1:
            z_send(a, 1, src).start()
        pltpu.make_async_copy(src, gathered[a].at[block_rows(0, 0)], keep.at[a]).start()

    def forward(a, dz, src):
        z_send(a, dz, src).wait_recv()
        for dx in range(1, x_n):
            x_send(a, dz, dx, gathered[a].at[block_rows(dz, 0)]).start()
        if dz + 1 < z_n:
            z_send(a, dz + 1, src).start()

    begin(0, cotangent)

    floats = inputs[...].astype(jnp.float32)
    lane = lax.broadcasted_iota(jnp.int32, (block, LANES), 1)

    def pair(first, second):
        return jnp.where(lane == 0, first, jnp.where(lane == 1, second, 0.0))

    def exchange(use):
        for step in range(1, rows):
            remote(
                stats.at[use, 0], stats.at[use, step], st_s.at[use, step], st_r.at[use, step],
                (lax.rem(row + step, rows), col),
            ).start()
        total = stats[use, 0]
        for step in range(1, rows):
            remote(
                stats.at[use, 0], stats.at[use, step], st_s.at[use, step], st_r.at[use, step],
                (lax.rem(row + step, rows), col),
            ).wait()
            total = total + stats[use, step]
        total = total / width
        return (
            jnp.sum(jnp.where(lane == 0, total, 0.0), axis=1, keepdims=True),
            jnp.sum(jnp.where(lane == 1, total, 0.0), axis=1, keepdims=True),
        )

    stats[0, 0] = pair(jnp.sum(floats, axis=1, keepdims=True), jnp.sum(floats * floats, axis=1, keepdims=True))
    center, meansq = exchange(0)
    spread = lax.rsqrt(meansq - center * center + epsilon)
    sums[0] = jnp.broadcast_to(center, (block, LANES))
    sums[1] = jnp.broadcast_to(spread, (block, LANES))
    scaled[...] = ((floats - center) * spread * gain[...]).astype(jnp.bfloat16)
    begin(1, scaled)

    def core_copy(a, g):
        return remote(
            part.at[a, g, pl.ds(pl.multiple_of((1 - core) * half, half), half)], core_in.at[a, g],
            rc_s.at[a, g], rc_r.at[a, g], other_core,
        )

    def y_copy(a, g, step):
        start = core * half + lax.rem(y + step, y_n) * quarter
        return remote(
            part.at[a, g, pl.ds(pl.multiple_of(start, quarter), quarter)], y_in.at[a, g, step - 1],
            ry_s.at[a, g, step], ry_r.at[a, g, step], at_y(step),
        )

    def multiply(right, dims, out_cols, store):
        tile = tile_of(out_cols)

        @pl.loop(0, out_cols // tile)
        def _(n):
            here = pl.ds(pl.multiple_of(n * tile, tile), tile)
            left = lhs[...] if store[2] == ff else lhs[:, :d]
            piece = right[here, :] if dims is ROWS_ROWS else right[:, here]
            value = lax.dot_general(left, piece, dims, preferred_element_type=jnp.float32).astype(jnp.bfloat16)
            a, g, _, offset = store
            part[a, g, :, pl.ds(pl.multiple_of(offset + n * tile, LANES), tile)] = value

    own_blocks = (cotangent, scaled)

    def project(a, g):
        if g == 0:
            pltpu.make_async_copy(own_blocks[a], gathered[a].at[block_rows(0, 0)], keep.at[a]).wait()
            weight_loads[a].wait()
        for dx in range(1, x_n):
            x_send(a, g, dx, own_blocks[a]).wait_recv()
        take(gathered[a].at[pl.ds(g * tokens, tokens)], lhs.at[:, pl.ds(0, d)])
        multiply(w_out if a == 0 else w_in, ROWS_ROWS if a == 0 else ROWS_COLS, ff, (a, g, d, 0))
        core_copy(a, g).start()

    def core_sum(a, g):
        core_copy(a, g).wait()
        mine = pl.ds(pl.multiple_of(core * half, half), half)
        tile = tile_of(ff)

        @pl.loop(0, ff // tile)
        def _(n):
            here = pl.ds(pl.multiple_of(n * tile, tile), tile)
            total = part[a, g, mine, here].astype(jnp.float32) + core_in[a, g, :, here].astype(jnp.float32)
            part[a, g, mine, here] = total.astype(jnp.bfloat16)

        for step in range(1, y_n):
            y_copy(a, g, step).start()

    def share_copy(a, g, step):
        start = g * tokens + core * half + y * quarter
        return remote(
            own.at[a, g], spread_out[a].at[pl.ds(pl.multiple_of(start, quarter), quarter)],
            ay_s.at[a, g, step], ay_r.at[a, g, step], at_y(step),
        )

    def share_keep(a, g):
        start = g * tokens + core * half + y * quarter
        return pltpu.make_async_copy(
            own.at[a, g], spread_out[a].at[pl.ds(pl.multiple_of(start, quarter), quarter)], ay_s.at[a, g, 0]
        )

    def activate(g):
        for a in range(2):
            for step in range(1, y_n):
                y_copy(a, g, step).wait()
        mine = pl.ds(pl.multiple_of(core * half + y * quarter, quarter), quarter)
        tile = tile_of(ff)

        @pl.loop(0, ff // tile)
        def _(n):
            here = pl.ds(pl.multiple_of(n * tile, tile), tile)
            back = part[0, g, mine, here].astype(jnp.float32)
            hidden = part[1, g, mine, here].astype(jnp.float32)
            for step in range(y_n - 1):
                back = back + y_in[0, g, step, :, here].astype(jnp.float32)
                hidden = hidden + y_in[1, g, step, :, here].astype(jnp.float32)
            cdf = 0.5 * (1.0 + lax.erf(hidden * ROOT_HALF))
            density = jnp.exp(-0.5 * hidden * hidden) * ROOT_TWO_PI
            own[0, g, :, here] = (hidden * cdf).astype(jnp.bfloat16)
            own[1, g, :, here] = (back * (cdf + hidden * density)).astype(jnp.bfloat16)

        for step in range(1, y_n):
            share_copy(0, g, step).start()
        for a in range(2):
            share_keep(a, g).start()

    def half_copy(a, g):
        here = pl.ds(pl.multiple_of(g * tokens + core * half, half), half)
        return remote(spread_out[a].at[here], spread_out[a].at[here], ac_s.at[a, g], ac_r.at[a, g], other_core)

    def pass_on(a, g):
        for step in range(1, y_n):
            share_copy(a, g, step).wait()
        if a == 0:
            for step in range(1, y_n):
                share_copy(1, g, step).start()
        share_keep(a, g).wait()
        half_copy(a, g).start()

    def x_copy(a, g, dx):
        return remote(
            part.at[0, g, pl.ds(dx * block, block), pl.ds(a * d, d)], x_in.at[a, g, dx - 1],
            xs_s.at[a, g, dx], xs_r.at[a, g, dx], at_x(dx),
        )

    def z_copy(a, g):
        return remote(
            part.at[0, g, pl.ds(0, block), pl.ds(a * d, d)], z_in.at[a, g - 1], zs_s.at[a, g], zs_r.at[a, g], at_z(g)
        )

    def finish(a, g):
        half_copy(a, g).wait()
        take(spread_out[a].at[pl.ds(g * tokens, tokens)], lhs)
        multiply(w_out if a == 0 else w_in, ROWS_COLS if a == 0 else ROWS_ROWS, d, (0, g, ff, a * d))
        for dx in range(1, x_n):
            x_copy(a, g, dx).start()

    def x_sum(a, g):
        for dx in range(1, x_n):
            x_copy(a, g, dx).wait()
        if x_n > 1:
            total = part[0, g, :block, a * d : (a + 1) * d].astype(jnp.float32)
            for dx in range(1, x_n):
                total = total + x_in[a, g, dx - 1].astype(jnp.float32)
            part[0, g, :block, a * d : (a + 1) * d] = total.astype(jnp.bfloat16)
        if g:
            z_copy(a, g).start()

    last = z_n - 1
    for step in range(z_n + 3):
        if step >= 2 and step - 2 < last:
            pass_on(0, step - 2)
        if step != 1 and step != 3 and 0 <= step - 1 < z_n:
            activate(step - 1)
        if 0 <= step - 3 < z_n:
            pass_on(1, step - 3)
            if step - 3 < last:
                finish(0, step - 3)
                if step - 3 == last - 1:
                    pass_on(0, last)
            finish(1, step - 3)
        for a in range(2):
            if 0 <= step - 4 < last - 1:
                x_sum(a, step - 4)
        if step == z_n + 1:
            finish(0, last)
            for a in range(2):
                x_sum(a, last - 1)
        for a in range(2):
            if step < z_n:
                project(a, step)
                core_sum(a, step)
                if step != 1 and step + 1 < z_n:
                    forward(a, step + 1, own_blocks[a])
        if step in (1, 3) and step - 1 < z_n:
            activate(step - 1)
        if step == 1 and step + 1 < z_n:
            for a in range(2):
                forward(a, step + 1, own_blocks[a])
    for a in range(2):
        x_sum(a, last)

    def collected(a):
        total = part[0, 0, :block, a * d : (a + 1) * d].astype(jnp.float32)
        for g in range(1, z_n):
            z_copy(a, g).wait()
            total = total + z_in[a, g - 1].astype(jnp.float32)
        return total

    normed_gradient = collected(1)
    normed = (inputs[...].astype(jnp.float32) - sums[0][:, :1]) * sums[1][:, :1]
    products = jnp.sum(normed_gradient * normed, axis=0, keepdims=True)
    for n in range(d // LANES):
        gains[0, n : n + 1, :] = products[:, n * LANES : (n + 1) * LANES]

    def gain_copy(step):
        return remote(gains.at[0], gains.at[step], gn_s.at[step], gn_r.at[step], (row, lax.rem(col + step, cols)))

    for step in range(1, cols):
        gain_copy(step).start()
    scaled_gradient = normed_gradient * gain[...]
    stats[1, 0] = pair(
        jnp.sum(scaled_gradient, axis=1, keepdims=True), jnp.sum(scaled_gradient * normed, axis=1, keepdims=True)
    )
    mean_gradient, mean_cross = exchange(1)
    input_gradient[...] = (sums[1][:, :1] * (scaled_gradient - mean_gradient - normed * mean_cross)).astype(jnp.bfloat16)
    branch[...] = collected(0).astype(jnp.bfloat16)
    total = gains[0]
    for step in range(1, cols):
        gain_copy(step).wait()
        total = total + gains[step]
    gain_gradient[...] = total
    for a in range(2):
        for dz in range(z_n):
            for dx in range(x_n):
                if dx:
                    x_send(a, dz, dx, own_blocks[a]).wait_send()
                elif dz:
                    z_send(a, dz, own_blocks[a]).wait_send()


def make_per_device(rows, cols):
    y_n = rows // CORES
    z_n = 4 if cols % 4 == 0 else 1
    x_n = cols // z_n

    def per_device(inputs, norm_gain, weight_in, weight_out, cotangent):
        block, d = inputs.shape
        ff = weight_in.shape[1]
        tokens = x_n * block
        half = tokens // CORES
        quarter = half // y_n
        every = z_n * tokens
        bf16, f32 = jnp.bfloat16, jnp.float32
        dma = pltpu.SemaphoreType.DMA
        vmem = pl.BlockSpec(memory_space=pltpu.VMEM)
        anywhere = pl.BlockSpec(memory_space=pl.ANY)

        def shape(*dims, dtype=bf16):
            return jax.ShapeDtypeStruct(dims, dtype)

        outs = pl.pallas_call(
            functools.partial(layer_kernel, rows, y_n, z_n, x_n),
            out_shape=(
                shape(block, d), shape(block, d), shape(d // LANES, LANES, dtype=f32),
                shape(every, d), shape(every, d), shape(every, ff), shape(every, ff),
            ),
            in_specs=[vmem, vmem, anywhere, anywhere, anywhere],
            out_specs=(vmem, vmem, vmem, anywhere, anywhere, anywhere, anywhere),
            scratch_shapes=[
                pltpu.VMEM((d, ff), bf16),
                pltpu.VMEM((ff, d), bf16),
                pltpu.VMEM((2, z_n, tokens, ff), bf16),
                pltpu.VMEM((2, z_n, half, ff), bf16),
                pltpu.VMEM((2, z_n, max(y_n - 1, 1), quarter, ff), bf16),
                pltpu.VMEM((2, z_n, quarter, ff), bf16),
                pltpu.VMEM((tokens, ff), bf16),
                pltpu.VMEM((2, z_n, max(x_n - 1, 1), block, d), bf16),
                pltpu.VMEM((2, max(z_n - 1, 1), block, d), bf16),
                pltpu.VMEM((block, d), bf16),
                pltpu.VMEM((2, rows, block, LANES), f32),
                pltpu.VMEM((2, block, LANES), f32),
                pltpu.VMEM((cols, d // LANES, LANES), f32),
                dma((2, z_n, x_n)), dma((2, z_n, x_n)),
                dma((2, z_n)), dma((2, z_n)),
                dma((2, z_n, y_n)), dma((2, z_n, y_n)),
                dma((2, z_n, y_n)), dma((2, z_n, y_n)),
                dma((2, z_n)), dma((2, z_n)),
                dma((2, z_n, x_n)), dma((2, z_n, x_n)),
                dma((2, z_n)), dma((2, z_n)),
                dma((2, rows)), dma((2, rows)),
                dma((cols,)), dma((cols,)),
                dma, dma((2,)), dma((2,)),
            ],
            compiler_params=pltpu.CompilerParams(
                collective_id=0, has_side_effects=True, vmem_limit_bytes=62 * 1024 * 1024
            ),
            cost_estimate=pl.CostEstimate(
                flops=8 * every * d * ff, bytes_accessed=8 * d * ff, transcendentals=2 * every * ff // rows
            ),
        )(inputs, norm_gain[None, :], weight_in, weight_out, cotangent)
        branch, input_gradient, gain_gradient, cot_all, scl_all, act_all, slo_all = outs
        over_tokens = (((0,), (0,)), ((), ()))
        out_gradient = lax.dot_general(act_all, cot_all, over_tokens, preferred_element_type=f32)
        in_gradient = lax.dot_general(scl_all, slo_all, over_tokens, preferred_element_type=f32)
        return branch, input_gradient, in_gradient, out_gradient, gain_gradient.reshape(-1)

    return per_device


def solution(mesh):
    in_specs = (P("col", "row"), P("row"), P("row", "col"), P("col", "row"), P("col", "row"))
    out_specs = (P("col", "row"), P("col", "row"), P("row", "col"), P("col", "row"), P("row"))
    per_device = make_per_device(mesh.shape["row"], mesh.shape["col"])
    return jax.shard_map(per_device, mesh=mesh, in_specs=in_specs, out_specs=out_specs, check_vma=False)
```

```python
import functools

import jax
import jax.numpy as jnp
from jax import lax
from jax.experimental import pallas as pl
from jax.experimental.pallas import tpu as pltpu
from jax.sharding import PartitionSpec as P

MESH = pl.DeviceIdType.MESH
CORES = 2
LANES = 128
epsilon = 1e-06
ROOT_HALF = 0.7071067811865476
ROOT_TWO_PI = 0.3989422804014327
ROWS_ROWS = (((1,), (1,)), ((), ()))
ROWS_COLS = (((1,), (0,)), ((), ()))


def tile_of(size):
    return 512 if size % 512 == 0 else 256 if size % 256 == 0 else 128


def wide_tile_of(size):
    return next((tile for tile in (1024, 768, 512, 256) if size % tile == 0), LANES)


def layer_kernel(
    rows, y_n, z_n, x_n,
    inputs, gain, weight_in, weight_out, cotangent,
    branch, input_gradient, gain_gradient, cot_all, scl_all, act_all, slo_all,
    w_in, w_out, part, core_in, y_in, own, lhs, x_in, z_in, scaled, stats, sums, gains,
    ag_s, ag_r, rc_s, rc_r, ry_s, ry_r, ay_s, ay_r, ac_s, ac_r, xs_s, xs_r, zs_s, zs_r,
    st_s, st_r, gn_s, gn_r, load, wload, keep,
):
    block, d = inputs.shape
    ff = w_in.shape[1]
    tokens = x_n * block
    half = tokens // CORES
    quarter = half // y_n
    cols = z_n * x_n
    width = d * rows
    row = lax.axis_index("row")
    col = lax.axis_index("col")
    y, core = row // CORES, row % CORES
    z, x = col // x_n, col % x_n

    def at_z(step):
        return (row, lax.rem(z + step + z_n, z_n) * x_n + x)

    def at_x(step):
        return (row, z * x_n + lax.rem(x + step + x_n, x_n))

    def at_y(step):
        return (lax.rem(y + step, y_n) * CORES + core, col)

    other_core = (y * CORES + 1 - core, col)

    def remote(src, dst, send, recv, device):
        return pltpu.make_async_remote_copy(
            src_ref=src, dst_ref=dst, send_sem=send, recv_sem=recv, device_id=device, device_id_type=MESH
        )

    barrier = pltpu.get_barrier_semaphore()
    for step in range(1, rows):
        pl.semaphore_signal(barrier, inc=1, device_id=(lax.rem(row + step, rows), col), device_id_type=MESH)
    for step in range(1, cols):
        pl.semaphore_signal(barrier, inc=1, device_id=(row, lax.rem(col + step, cols)), device_id_type=MESH)
    weight_loads = [
        pltpu.make_async_copy(weight_out, w_out, wload.at[0]),
        pltpu.make_async_copy(weight_in, w_in, wload.at[1]),
    ]
    for copy in weight_loads:
        copy.start()
    pl.semaphore_wait(barrier, rows + cols - 2)

    gathered = (cot_all, scl_all)
    spread_out = (act_all, slo_all)

    def block_rows(dz, dx):
        return pl.ds(dz * tokens + dx * block, block)

    def z_send(a, dz, src):
        return remote(src, gathered[a].at[block_rows(dz, 0)], ag_s.at[a, dz, 0], ag_r.at[a, dz, 0], at_z(-dz))

    def x_send(a, dz, dx, src):
        return remote(src, gathered[a].at[block_rows(dz, dx)], ag_s.at[a, dz, dx], ag_r.at[a, dz, dx], at_x(-dx))

    def begin(a, src):
        for dx in range(1, x_n):
            x_send(a, 0, dx, src).start()
        if z_n > 1:
            z_send(a, 1, src).start()
        pltpu.make_async_copy(src, gathered[a].at[block_rows(0, 0)], keep.at[a]).start()

    def forward(a, dz, src):
        z_send(a, dz, src).wait_recv()
        for dx in range(1, x_n):
            x_send(a, dz, dx, gathered[a].at[block_rows(dz, 0)]).start()
        if dz + 1 < z_n:
            z_send(a, dz + 1, src).start()

    begin(0, cotangent)

    floats = inputs[...].astype(jnp.float32)
    lane = lax.broadcasted_iota(jnp.int32, (block, LANES), 1)

    def pair(first, second):
        return jnp.where(lane == 0, first, jnp.where(lane == 1, second, 0.0))

    def exchange(use):
        for step in range(1, rows):
            remote(
                stats.at[use, 0], stats.at[use, step], st_s.at[use, step], st_r.at[use, step],
                (lax.rem(row + step, rows), col),
            ).start()
        total = stats[use, 0]
        for step in range(1, rows):
            remote(
                stats.at[use, 0], stats.at[use, step], st_s.at[use, step], st_r.at[use, step],
                (lax.rem(row + step, rows), col),
            ).wait()
            total = total + stats[use, step]
        total = total / width
        return (
            jnp.sum(jnp.where(lane == 0, total, 0.0), axis=1, keepdims=True),
            jnp.sum(jnp.where(lane == 1, total, 0.0), axis=1, keepdims=True),
        )

    stats[0, 0] = pair(jnp.sum(floats, axis=1, keepdims=True), jnp.sum(floats * floats, axis=1, keepdims=True))
    center, meansq = exchange(0)
    spread = lax.rsqrt(meansq - center * center + epsilon)
    sums[0] = jnp.broadcast_to(center, (block, LANES))
    sums[1] = jnp.broadcast_to(spread, (block, LANES))
    scaled[...] = ((floats - center) * spread * gain[...]).astype(jnp.bfloat16)
    begin(1, scaled)

    def core_copy(a, g):
        return remote(
            part.at[a, g, pl.ds(pl.multiple_of((1 - core) * half, half), half)], core_in.at[a, g],
            rc_s.at[a, g], rc_r.at[a, g], other_core,
        )

    def y_copy(a, g, step):
        start = core * half + lax.rem(y + step, y_n) * quarter
        return remote(
            part.at[a, g, pl.ds(pl.multiple_of(start, quarter), quarter)], y_in.at[a, g, step - 1],
            ry_s.at[a, g, step], ry_r.at[a, g, step], at_y(step),
        )

    def multiply(right, dims, out_cols, slot, store):
        tile = wide_tile_of(out_cols)

        @pl.loop(0, out_cols // tile)
        def _(n):
            here = pl.ds(pl.multiple_of(n * tile, tile), tile)
            left = lhs[slot, :, : store[2]]
            piece = right[here, :] if dims is ROWS_ROWS else right[:, here]
            value = lax.dot_general(left, piece, dims, preferred_element_type=jnp.float32).astype(jnp.bfloat16)
            a, g, _, offset = store
            part[a, g, :, pl.ds(pl.multiple_of(offset + n * tile, LANES), tile)] = value

    own_blocks = (cotangent, scaled)

    def chunk_load(a, g):
        return pltpu.make_async_copy(gathered[a].at[pl.ds(g * tokens, tokens)], lhs.at[a, :, pl.ds(0, d)], load.at[a])

    def project_load(a, g):
        if g == 0:
            pltpu.make_async_copy(own_blocks[a], gathered[a].at[block_rows(0, 0)], keep.at[a]).wait()
        for dx in range(1, x_n):
            x_send(a, g, dx, own_blocks[a]).wait_recv()
        chunk_load(a, g).start()

    def project(a, g):
        if g == 0:
            weight_loads[a].wait()
        chunk_load(a, g).wait()
        multiply(w_out if a == 0 else w_in, ROWS_ROWS if a == 0 else ROWS_COLS, ff, a, (a, g, d, 0))
        core_copy(a, g).start()

    def core_sum(a, g):
        core_copy(a, g).wait()
        mine = pl.ds(pl.multiple_of(core * half, half), half)
        tile = tile_of(ff)

        @pl.loop(0, ff // tile)
        def _(n):
            here = pl.ds(pl.multiple_of(n * tile, tile), tile)
            total = part[a, g, mine, here].astype(jnp.float32) + core_in[a, g, :, here].astype(jnp.float32)
            part[a, g, mine, here] = total.astype(jnp.bfloat16)

        for step in range(1, y_n):
            y_copy(a, g, step).start()

    def share_copy(a, g, step):
        start = g * tokens + core * half + y * quarter
        return remote(
            own.at[a, g], spread_out[a].at[pl.ds(pl.multiple_of(start, quarter), quarter)],
            ay_s.at[a, g, step], ay_r.at[a, g, step], at_y(step),
        )

    def share_keep(a, g):
        start = g * tokens + core * half + y * quarter
        return pltpu.make_async_copy(
            own.at[a, g], spread_out[a].at[pl.ds(pl.multiple_of(start, quarter), quarter)], ay_s.at[a, g, 0]
        )

    def activate(g):
        for a in range(2):
            for step in range(1, y_n):
                y_copy(a, g, step).wait()
        mine = pl.ds(pl.multiple_of(core * half + y * quarter, quarter), quarter)
        tile = tile_of(ff)

        @pl.loop(0, ff // tile)
        def _(n):
            here = pl.ds(pl.multiple_of(n * tile, tile), tile)
            back = part[0, g, mine, here].astype(jnp.float32)
            hidden = part[1, g, mine, here].astype(jnp.float32)
            for step in range(y_n - 1):
                back = back + y_in[0, g, step, :, here].astype(jnp.float32)
                hidden = hidden + y_in[1, g, step, :, here].astype(jnp.float32)
            cdf = 0.5 * (1.0 + lax.erf(hidden * ROOT_HALF))
            density = jnp.exp(-0.5 * hidden * hidden) * ROOT_TWO_PI
            own[0, g, :, here] = (hidden * cdf).astype(jnp.bfloat16)
            own[1, g, :, here] = (back * (cdf + hidden * density)).astype(jnp.bfloat16)

        for step in range(1, y_n):
            share_copy(0, g, step).start()
        for a in range(2):
            share_keep(a, g).start()

    def half_copy(a, g):
        here = pl.ds(pl.multiple_of(g * tokens + core * half, half), half)
        return remote(spread_out[a].at[here], spread_out[a].at[here], ac_s.at[a, g], ac_r.at[a, g], other_core)

    def pass_on(a, g):
        for step in range(1, y_n):
            share_copy(a, g, step).wait()
        if a == 0:
            for step in range(1, y_n):
                share_copy(1, g, step).start()
        share_keep(a, g).wait()
        half_copy(a, g).start()

    def x_copy(a, g, dx):
        return remote(
            part.at[0, g, pl.ds(dx * block, block), pl.ds(a * d, d)], x_in.at[a, g, dx - 1],
            xs_s.at[a, g, dx], xs_r.at[a, g, dx], at_x(dx),
        )

    def z_copy(a, g):
        return remote(
            part.at[0, g, pl.ds(0, block), pl.ds(a * d, d)], z_in.at[a, g - 1], zs_s.at[a, g], zs_r.at[a, g], at_z(g)
        )

    def finish_copy(a, g):
        return pltpu.make_async_copy(spread_out[a].at[pl.ds(g * tokens, tokens)], lhs.at[a], load.at[a])

    def finish_load(a, g):
        half_copy(a, g).wait()
        finish_copy(a, g).start()

    def finish(a, g):
        finish_copy(a, g).wait()
        multiply(w_out if a == 0 else w_in, ROWS_COLS if a == 0 else ROWS_ROWS, d, a, (0, g, ff, a * d))
        for dx in range(1, x_n):
            x_copy(a, g, dx).start()

    def x_sum(a, g):
        for dx in range(1, x_n):
            x_copy(a, g, dx).wait()
        if x_n > 1:
            total = part[0, g, :block, a * d : (a + 1) * d].astype(jnp.float32)
            for dx in range(1, x_n):
                total = total + x_in[a, g, dx - 1].astype(jnp.float32)
            part[0, g, :block, a * d : (a + 1) * d] = total.astype(jnp.bfloat16)
        if g:
            z_copy(a, g).start()

    last = z_n - 1

    def both(action, g):
        if 0 <= g < z_n:
            for a in range(2):
                action(a, g)

    def project_both(g):
        if g < z_n:
            both(project_load, g)
            if g >= 2:
                forward_both(g + 1)
            both(project, g)
            both(core_sum, g)

    def finish_both(g):
        both(finish_load, g)
        both(finish, g)

    def forward_both(g):
        if g < z_n:
            for a in range(2):
                forward(a, g, own_blocks[a])

    for a in range(2):
        project_load(a, 0)
        project(a, 0)
        if last:
            forward(a, 1, own_blocks[a])
    both(core_sum, 0)
    for step in range(1, z_n + 1):
        if step >= 2:
            pass_on(0, step - 2)
        if step == 2:
            activate(step - 1)
        project_both(step)
        if step >= 3:
            pass_on(1, step - 3)
        if step != 2:
            activate(step - 1)
        if step == 1:
            forward_both(2)
        if step >= 3:
            finish_both(step - 3)
        both(x_sum, step - 4)
    pass_on(0, last)
    if last >= 1:
        pass_on(1, last - 1)
        both(x_sum, last - 2)
        finish_both(last - 1)
    finish_load(0, last)
    finish(0, last)
    both(x_sum, last - 1)
    pass_on(1, last)
    x_sum(0, last)
    finish_load(1, last)
    finish(1, last)
    x_sum(1, last)

    def collected(a):
        total = part[0, 0, :block, a * d : (a + 1) * d].astype(jnp.float32)
        for g in range(1, z_n):
            z_copy(a, g).wait()
            total = total + z_in[a, g - 1].astype(jnp.float32)
        return total

    normed_gradient = collected(1)
    normed = (inputs[...].astype(jnp.float32) - sums[0][:, :1]) * sums[1][:, :1]
    products = jnp.sum(normed_gradient * normed, axis=0, keepdims=True)
    for n in range(d // LANES):
        gains[0, n : n + 1, :] = products[:, n * LANES : (n + 1) * LANES]

    def gain_copy(step):
        return remote(gains.at[0], gains.at[step], gn_s.at[step], gn_r.at[step], (row, lax.rem(col + step, cols)))

    for step in range(1, cols):
        gain_copy(step).start()
    scaled_gradient = normed_gradient * gain[...]
    stats[1, 0] = pair(
        jnp.sum(scaled_gradient, axis=1, keepdims=True), jnp.sum(scaled_gradient * normed, axis=1, keepdims=True)
    )
    mean_gradient, mean_cross = exchange(1)
    input_gradient[...] = (sums[1][:, :1] * (scaled_gradient - mean_gradient - normed * mean_cross)).astype(jnp.bfloat16)
    branch[...] = collected(0).astype(jnp.bfloat16)
    total = gains[0]
    for step in range(1, cols):
        gain_copy(step).wait()
        total = total + gains[step]
    gain_gradient[...] = total
    for a in range(2):
        for dz in range(z_n):
            for dx in range(x_n):
                if dx:
                    x_send(a, dz, dx, own_blocks[a]).wait_send()
                elif dz:
                    z_send(a, dz, own_blocks[a]).wait_send()


def make_per_device(rows, cols):
    y_n = rows // CORES
    z_n = 4 if cols % 4 == 0 else 1
    x_n = cols // z_n

    def per_device(inputs, norm_gain, weight_in, weight_out, cotangent):
        block, d = inputs.shape
        ff = weight_in.shape[1]
        tokens = x_n * block
        half = tokens // CORES
        quarter = half // y_n
        every = z_n * tokens
        bf16, f32 = jnp.bfloat16, jnp.float32
        dma = pltpu.SemaphoreType.DMA
        vmem = pl.BlockSpec(memory_space=pltpu.VMEM)
        anywhere = pl.BlockSpec(memory_space=pl.ANY)

        def shape(*dims, dtype=bf16):
            return jax.ShapeDtypeStruct(dims, dtype)

        outs = pl.pallas_call(
            functools.partial(layer_kernel, rows, y_n, z_n, x_n),
            out_shape=(
                shape(block, d), shape(block, d), shape(d // LANES, LANES, dtype=f32),
                shape(every, d), shape(every, d), shape(every, ff), shape(every, ff),
            ),
            in_specs=[vmem, vmem, anywhere, anywhere, anywhere],
            out_specs=(vmem, vmem, vmem, anywhere, anywhere, anywhere, anywhere),
            scratch_shapes=[
                pltpu.VMEM((d, ff), bf16),
                pltpu.VMEM((ff, d), bf16),
                pltpu.VMEM((2, z_n, tokens, ff), bf16),
                pltpu.VMEM((2, z_n, half, ff), bf16),
                pltpu.VMEM((2, z_n, max(y_n - 1, 1), quarter, ff), bf16),
                pltpu.VMEM((2, z_n, quarter, ff), bf16),
                pltpu.VMEM((2, tokens, ff), bf16),
                pltpu.VMEM((2, z_n, max(x_n - 1, 1), block, d), bf16),
                pltpu.VMEM((2, max(z_n - 1, 1), block, d), bf16),
                pltpu.VMEM((block, d), bf16),
                pltpu.VMEM((2, rows, block, LANES), f32),
                pltpu.VMEM((2, block, LANES), f32),
                pltpu.VMEM((cols, d // LANES, LANES), f32),
                dma((2, z_n, x_n)), dma((2, z_n, x_n)),
                dma((2, z_n)), dma((2, z_n)),
                dma((2, z_n, y_n)), dma((2, z_n, y_n)),
                dma((2, z_n, y_n)), dma((2, z_n, y_n)),
                dma((2, z_n)), dma((2, z_n)),
                dma((2, z_n, x_n)), dma((2, z_n, x_n)),
                dma((2, z_n)), dma((2, z_n)),
                dma((2, rows)), dma((2, rows)),
                dma((cols,)), dma((cols,)),
                dma((2,)), dma((2,)), dma((2,)),
            ],
            compiler_params=pltpu.CompilerParams(
                collective_id=0, has_side_effects=True, vmem_limit_bytes=62 * 1024 * 1024
            ),
            cost_estimate=pl.CostEstimate(
                flops=8 * every * d * ff, bytes_accessed=8 * d * ff, transcendentals=2 * every * ff // rows
            ),
        )(inputs, norm_gain[None, :], weight_in, weight_out, cotangent)
        branch, input_gradient, gain_gradient, cot_all, scl_all, act_all, slo_all = outs
        over_tokens = (((0,), (0,)), ((), ()))
        out_gradient = lax.dot_general(act_all, cot_all, over_tokens, preferred_element_type=f32)
        in_gradient = lax.dot_general(scl_all, slo_all, over_tokens, preferred_element_type=f32)
        return branch, input_gradient, in_gradient, out_gradient, gain_gradient.reshape(-1)

    return per_device


def solution(mesh):
    in_specs = (P("col", "row"), P("row"), P("row", "col"), P("col", "row"), P("col", "row"))
    out_specs = (P("col", "row"), P("col", "row"), P("row", "col"), P("col", "row"), P("row"))
    per_device = make_per_device(mesh.shape["row"], mesh.shape["col"])
    return jax.shard_map(per_device, mesh=mesh, in_specs=in_specs, out_specs=out_specs, check_vma=False)
```
